32 devices in a mesh: blk: 8 (over y, x, core), group: 4 (over z).
Axes of the slice: x: 2, y: 2, z: 4, core: 2. Of those that a mesh axis runs over, the one named last changes fastest.
Arguments:
- centres: bfloat16 [65536, 1024], P(('blk', 'group')), may hold values from -8 to 8
- batch_x: bfloat16 [512, 1024], P(('blk', 'group')), may hold values from -8 to 8
- grad: bfloat16 [512, 1000], P(('blk', 'group')), may hold values from -0.29882812 to 0.29882812
- eigvec: float32 [16384, 128], P(('blk', 'group')), may hold values from -0.046875 to 0.046875
- eig_scale: float32 [128], replicated, may hold values from 2 to 20
- sub_index: int32 [16384], P(('blk', 'group')), may hold values from 0 to 65535, as said below
Outputs:
- update: float32 [65536, 1000], P(('blk', 'group'))
The draws below stay inside these ranges and needn't reach their ends.
Inputs may be any that keep to these rules, and one draw needn't show every extreme that they name: `sub_index`: all entries are distinct. Entry i of the block of 512 entries that device index k of blk+group holds names a centre among rows (k // 4) * 4 * 2048 to (k // 4 + 1) * 4 * 2048 - 1; among one such block at most 128 entries name rows of any one aligned run of 2048 centres, and every block has exactly 128 in one run.
All inputs are finite; a program needn't handle non-finite values.
Results may differ from the reference program's by a relative error of at most 0.0027.
Values may be sent and summed in bfloat16 or wider, within the bound.
A program may use at most 128 MiB of HBM per device.

```python
import math
import jax
import jax.numpy as jnp
from jax import lax

D = 1024
CLS = 1000
Q = 128
C_DEV = 2048
NYS_DEV = 512
CAP = 128
CENT = 65536
BATCH = 512
NYS = 16384
CLUST = 64
N_BLK = 8
N_GROUP = 4


def cluster_points(key, count, salt):
    means_key = jax.random.fold_in(key, 101)
    means = 1.5 * jax.random.truncated_normal(means_key, -4.0, 4.0, (CLUST, D), jnp.float32)
    labels = jax.random.randint(jax.random.fold_in(key, salt), (count,), 0, CLUST)
    noise_key = jax.random.fold_in(key, salt + 1)
    noise = 0.4 * jax.random.truncated_normal(noise_key, -4.0, 4.0, (count, D), jnp.float32)
    return (means[labels] + noise).astype(jnp.bfloat16)


def draw_centres(key, part):
    return cluster_points(key, CENT, 202)


def draw_batch_x(key, part):
    return cluster_points(key, BATCH, 303)


def draw_sub_index(key, part):
    count = N_BLK * N_GROUP
    perm_keys = jax.random.split(jax.random.fold_in(key, 11), count)
    perm_table = jax.vmap(lambda k: jax.random.permutation(k, C_DEV))(perm_keys)
    owner_keys = jax.random.split(jax.random.fold_in(key, 23), count)

    def owner_rows(okey, device):
        key_first, key_pool, key_order = jax.random.split(okey, 3)
        first = jax.random.randint(key_first, (), 0, N_GROUP)
        pool = 1 + jnp.arange((N_GROUP - 1) * CAP, dtype=jnp.int32) // CAP
        pool = jax.random.permutation(key_pool, pool)[:NYS_DEV - CAP]
        offsets = jnp.concatenate([jnp.zeros((CAP,), jnp.int32), pool])
        offsets = jax.random.permutation(key_order, offsets)
        holder = (first + offsets) % N_GROUP
        onehot = (holder[:, None] == jnp.arange(N_GROUP, dtype=jnp.int32)[None, :]).astype(jnp.int32)
        order_in = jnp.sum(jnp.cumsum(onehot, axis=0) * onehot, axis=1) - 1
        slab = device // N_GROUP
        member = device % N_GROUP
        target = slab * N_GROUP + holder
        local_row = perm_table[target, member * CAP + order_in]
        return (target * C_DEV + local_row).astype(jnp.int32)
    devices = jnp.arange(count, dtype=jnp.int32)
    return jax.vmap(owner_rows)(owner_keys, devices).reshape(-1)


def block_levels(stream_key, shape, shards, low, high):
    level = 1.0
    for position, blocks in shards:
        steps = jax.random.uniform(jax.random.fold_in(jax.random.fold_in(stream_key, 6), position), (blocks,), jnp.float32, low / len(shards), high / len(shards))
        level = level * jnp.repeat(jnp.exp(steps), shape[position] // blocks).reshape((-1,) + (1,) * (len(shape) - 1 - position))
    return level


def gaussian(rng, dims, width, most, shards=(), kind=jnp.bfloat16):
    array = jax.random.normal(rng, dims, jnp.float32) * width
    if len(shards) > 0:
        array = block_levels(rng, dims, shards, -0.22, 0.18) * array
    return jnp.clip(array, min=-most, max=most).astype(kind)


def setup_inputs(seed: int = 0) -> dict:
    key_of = jax.random.split(jax.random.key(seed), 7)
    centres = draw_centres(jax.random.fold_in(key_of[6], 71), 0)
    batch_x = draw_batch_x(jax.random.fold_in(key_of[6], 71), 0)
    grad = gaussian(key_of[2], (BATCH, CLS), 0.05, 0.29882812, ((0, 32),))
    eigvec = gaussian(key_of[3], (NYS, Q), NYS ** -0.5, 0.046875, ((0, 32),), jnp.float32)
    eig_scale = jnp.clip(jnp.exp(jax.random.uniform(key_of[4], (Q,), jnp.float32, math.log(2.0), math.log(20.0))), 2.0, 20.0)
    sub_index = draw_sub_index(jax.random.fold_in(key_of[6], 71), 0)
    return {"centres": centres, "batch_x": batch_x, "grad": grad, "eigvec": eigvec, "eig_scale": eig_scale, "sub_index": sub_index}


def reference(centres, batch_x, grad, eigvec, eig_scale, sub_index):
    batch_sq = jnp.sum(jnp.square(batch_x.astype(jnp.float32)), axis=1)

    def centre_block(block_rows):
        centre_sq = jnp.sum(jnp.square(block_rows.astype(jnp.float32)), axis=1)
        inner_prod = jnp.dot(block_rows, batch_x.T, preferred_element_type=jnp.float32)
        distance = centre_sq[:, None] + batch_sq[None, :] - 2.0 * inner_prod
        kernel_tile = jnp.exp(-distance / (2.0 * D)).astype(jnp.bfloat16)
        return jnp.dot(kernel_tile, grad, preferred_element_type=jnp.float32)

    kernel_grad = lax.map(centre_block, centres.reshape(CENT // C_DEV, C_DEV, D)).reshape(CENT, CLS)
    picked = kernel_grad[sub_index]
    projected = jnp.dot(eigvec.T, picked, precision=lax.Precision.HIGHEST)
    correction = jnp.dot(eigvec * eig_scale[None, :], projected, precision=lax.Precision.HIGHEST)
    return kernel_grad.at[sub_index].add(-correction)
```

```python
import functools

import jax
import jax.numpy as jnp
from jax import lax
from jax.experimental import pallas as pl
from jax.experimental.pallas import tpu as pltpu
from jax.sharding import PartitionSpec as P

CAP = 128
TILE = 256
F32, BF16 = jnp.float32, jnp.bfloat16


def nt(a, b):
    return lax.dot_general(a, b, (((1,), (1,)), ((), ())), preferred_element_type=F32)


def split(a):
    hi = a.astype(BF16)
    return hi, (a - hi.astype(F32)).astype(BF16)


def onehot(a, b):
    return jnp.where(a == b, 1.0, 0.0).astype(BF16)


def copy_to(src, dst, send, recv, blk, grp):
    return pltpu.make_async_remote_copy(
        src_ref=src,
        dst_ref=dst,
        send_sem=send,
        recv_sem=recv,
        device_id=(blk, grp),
        device_id_type=pl.DeviceIdType.MESH,
    )


class Gather:
    def __init__(self, me, grid, own, whole, send, recv):
        self.me, self.grid, self.own, self.whole, self.send, self.recv = me, grid, own, whole, send, recv
        self.sent = []

    def push(self, src, slot, blk, grp):
        copy = copy_to(src, self.whole.at[slot], self.send.at[len(self.sent)], self.recv.at[slot], blk, grp)
        copy.start()
        self.sent.append(copy)

    def wait(self, slot):
        blk, grp = self.me
        there = self.whole.at[slot]
        copy_to(there, there, self.send.at[0], self.recv.at[slot], self.twin, grp).wait_recv()

    @property
    def twin(self):
        blk, _ = self.me
        return blk + 1 - 2 * lax.rem(blk, 2)

    def chips(self):
        blk, _ = self.me
        n = self.grid[0] // 2
        core, chip = lax.rem(blk, 2), lax.div(blk, 2)
        return [2 * lax.rem(chip + k, n) + core for k in range(1, n)]

    def groups(self):
        _, grp = self.me
        return [lax.rem(grp + k, self.grid[1]) for k in range(1, self.grid[1])]

    def slot(self, blk, grp):
        return blk * self.grid[1] + grp

    def first(self):
        blk, grp = self.me
        slot = self.slot(blk, grp)
        self.whole[slot] = self.own[...]
        for other in self.groups():
            self.push(self.own, slot, blk, other)
        for other in self.chips():
            self.push(self.own, slot, other, grp)
        self.push(self.own, slot, self.twin, grp)

    def second(self):
        blk, grp = self.me
        for source in self.groups():
            slot = self.slot(blk, source)
            self.wait(slot)
            for other in self.chips():
                self.push(self.whole.at[slot], slot, other, grp)
            self.push(self.whole.at[slot], slot, self.twin, grp)

    def third(self):
        _, grp = self.me
        for source in [grp] + self.groups():
            for other in self.chips():
                slot = self.slot(other, source)
                self.wait(slot)
                self.push(self.whole.at[slot], slot, self.twin, grp)

    def last(self):
        _, grp = self.me
        n = self.grid[0] // 2
        core = lax.rem(self.twin, 2)
        for chip in range(n):
            for source in range(self.grid[1]):
                self.wait(self.slot(2 * chip + core, source))

    def drain(self):
        for copy in self.sent:
            copy.wait_send()


def exchange(
    grid, x_ref, g_ref, vec_ref, scale_ref, index_ref, c_hbm, gp_ref, rhs_ref,
    xall, gall, cbuf, csq, vec_out, vec_in, row_out, row_in, acc,
    part, part_in, some, some_in, full,
    c_sem, x_send, x_recv, g_send, g_recv, v_send, v_recv, r_send, r_recv,
    p_send, p_recv, s_send, s_recv, f_send, f_recv,
):
    n_blk, n_grp = grid
    blk, grp = lax.axis_index("blk"), lax.axis_index("group")
    n_rows, dim = cbuf.shape
    subs = vec_ref.shape[0]
    q = vec_ref.shape[1]
    batch = xall.shape[0] * xall.shape[1]
    piece = batch // n_blk
    classes = g_ref.shape[1]
    tiles = n_rows // TILE

    load = pltpu.make_async_copy(c_hbm, cbuf, c_sem)
    load.start()

    other_grps = [lax.rem(grp + k, n_grp) for k in range(1, n_grp)]
    other_blks = [lax.rem(blk + k, n_blk) for k in range(1, n_blk)]
    barrier = pltpu.get_barrier_semaphore()
    for other in other_grps:
        pl.semaphore_signal(barrier, inc=1, device_id=(blk, other), device_id_type=pl.DeviceIdType.MESH)
    for other in other_blks:
        pl.semaphore_signal(barrier, inc=1, device_id=(other, grp), device_id_type=pl.DeviceIdType.MESH)
    pl.semaphore_wait(barrier, n_grp + n_blk - 2)

    xs = Gather((blk, grp), grid, x_ref, xall, x_send, x_recv)
    gs = Gather((blk, grp), grid, g_ref, gall, g_send, g_recv)
    xs.first()

    index = jnp.broadcast_to(index_ref[...], (8, subs))
    shift = n_rows.bit_length() - 1
    local = index & (n_rows - 1)
    holder = lax.shift_right_logical(index, shift) & (n_grp - 1)
    line = lax.broadcasted_iota(jnp.int32, (8, subs), 0)
    member = jnp.where(holder == line, 1.0, 0.0)
    upper = jnp.where(
        lax.broadcasted_iota(jnp.int32, (subs, subs), 0) < lax.broadcasted_iota(jnp.int32, (subs, subs), 1), 1.0, 0.0
    ).astype(BF16)
    order = jnp.sum(member * jnp.dot(member.astype(BF16), upper, preferred_element_type=F32), axis=0, keepdims=True)
    position = holder[0:1].astype(F32) * CAP + order
    places = n_grp * CAP
    select = onehot(lax.broadcasted_iota(jnp.int32, (places, subs), 0).astype(F32), position)
    vec_hi, vec_lo = split(vec_ref[...])
    table = jnp.dot(select, jnp.concatenate([vec_hi, vec_lo], axis=1), preferred_element_type=F32).T
    wanted = jnp.where(line == 0, lax.shift_right_logical(local, 7), jnp.where(line == 1, local & 127, 1))
    rows = nt(wanted.astype(F32).astype(BF16), select)
    for k in range(n_grp):
        vec_out[k] = table[:, k * CAP : (k + 1) * CAP].astype(BF16)
        row_out[k] = rows[:, k * CAP : (k + 1) * CAP]
    vecs = []
    for k, other in enumerate(other_grps):
        vecs.append(copy_to(vec_out.at[other], vec_in.at[grp], v_send.at[k], v_recv.at[grp], blk, other))
        vecs.append(copy_to(row_out.at[other], row_in.at[grp], r_send.at[k], r_recv.at[grp], blk, other))
    for copy in vecs:
        copy.start()
    vec_in[grp] = vec_out[grp]
    row_in[grp] = row_out[grp]

    xs.second()
    gs.first()

    load.wait()
    ones = jnp.ones((8, 128), BF16)

    @pl.loop(0, tiles)
    def _(t):
        block = cbuf[pl.ds(pl.multiple_of(t * TILE, TILE), TILE), :].astype(F32)
        square = block * block
        total = square[:, :128]
        for k in range(1, dim // 128):
            total = total + square[:, k * 128 : (k + 1) * 128]
        hi = total.astype(BF16)
        mid, low = split(total - hi.astype(F32))
        csq[:, pl.ds(pl.multiple_of(t * TILE, TILE), TILE)] = nt(ones, hi) + nt(ones, mid) + nt(ones, low)

    xs.third()
    gs.second()

    for other in other_grps:
        copy_to(vec_in.at[other], vec_in.at[other], v_send.at[0], v_recv.at[other], blk, other).wait_recv()
        copy_to(row_in.at[other], row_in.at[other], r_send.at[0], r_recv.at[other], blk, other).wait_recv()
    vec_all = jnp.concatenate([vec_in[k] for k in range(n_grp)], axis=1)
    rows = jnp.concatenate([row_in[k] for k in range(n_grp)], axis=1)
    place = rows[0:1] * 128.0 + rows[1:2] + (rows[2:3] - 1.0) * (2.0 * n_rows)

    @pl.loop(0, tiles)
    def _(t):
        where = (lax.broadcasted_iota(jnp.int32, (TILE, places), 0) + t * TILE).astype(F32)
        at_centres = nt(vec_all, onehot(where, place)).astype(BF16)
        columns = pl.ds(pl.multiple_of(t * TILE, TILE), TILE)
        rhs_ref[batch : batch + 2 * q, columns] = at_centres
        rhs_ref[batch + 2 * q :, columns] = at_centres[:q]

    xs.last()
    x = xall[...].reshape(batch, dim)
    xf = x.astype(F32)
    bsq = jnp.sum(xf * xf, axis=1, keepdims=True)
    acc[...] = jnp.zeros_like(acc)

    @pl.loop(0, tiles)
    def _(t):
        columns = pl.ds(pl.multiple_of(t * TILE, TILE), TILE)
        inner = nt(xall[...].reshape(batch, dim), cbuf[columns, :])
        distance = csq[0:1, columns] + bsq - 2.0 * inner
        kern = jnp.exp(distance * (-0.5 / dim)).astype(BF16)
        rhs_ref[0:batch, columns] = kern
        acc[...] += nt(kern, rhs_ref[batch : batch + 2 * q, columns])

    both = acc[:, :q] + acc[:, q:]
    for k in range(n_blk):
        part[k] = both[k * piece : (k + 1) * piece]
    parts = [
        copy_to(part.at[other], part_in.at[blk], p_send.at[k], p_recv.at[blk], other, grp)
        for k, other in enumerate(other_blks)
    ]
    for copy in parts:
        copy.start()
    part_in[blk] = part[blk]
    gs.third()
    for other in other_blks:
        copy_to(part_in.at[other], part_in.at[other], p_send.at[0], p_recv.at[other], other, grp).wait_recv()
    some[...] = functools.reduce(jnp.add, [part_in[k] for k in range(n_blk)])
    somes = [
        copy_to(some, some_in.at[grp], s_send.at[k], s_recv.at[grp], blk, other) for k, other in enumerate(other_grps)
    ]
    for copy in somes:
        copy.start()
    some_in[grp] = some[...]
    gs.last()
    gp_ref[0:batch] = gall[...].reshape(batch, classes)
    for other in other_grps:
        copy_to(some_in.at[other], some_in.at[other], s_send.at[0], s_recv.at[other], blk, other).wait_recv()
    full[blk] = functools.reduce(jnp.add, [some_in[k] for k in range(n_grp)])
    fulls = [
        copy_to(full.at[blk], full.at[blk], f_send.at[k], f_recv.at[blk], other, grp)
        for k, other in enumerate(other_blks)
    ]
    for copy in fulls:
        copy.start()
    for other in other_blks:
        copy_to(full.at[other], full.at[other], f_send.at[0], f_recv.at[other], other, grp).wait_recv()

    scaled = (full[...].reshape(batch, q) * scale_ref[...]).T
    hi, lo = split(scaled)
    product = jnp.dot(jnp.concatenate([hi, lo], axis=0), gp_ref[0:batch], preferred_element_type=F32)
    hi, lo = split(-(product[:q] + product[q:]))
    gp_ref[batch : batch + q] = hi
    gp_ref[batch + q : batch + 2 * q] = hi
    gp_ref[batch + 2 * q :] = lo

    xs.drain()
    gs.drain()
    for copy in vecs + parts + somes + fulls:
        copy.wait_send()


def body(grid, centres, batch_x, grad, eigvec, eig_scale, sub_index):
    n_blk, n_grp = grid
    n_dev = n_blk * n_grp
    n_rows, dim = centres.shape
    mine, classes = grad.shape
    subs, q = eigvec.shape
    batch = mine * n_dev
    piece = batch // n_blk
    dma = pltpu.SemaphoreType.DMA
    vmem = pl.BlockSpec(memory_space=pltpu.VMEM)
    gp, rhs = pl.pallas_call(
        functools.partial(exchange, grid),
        out_shape=(
            jax.ShapeDtypeStruct((batch + 3 * q, classes), BF16),
            jax.ShapeDtypeStruct((batch + 3 * q, n_rows), BF16),
        ),
        in_specs=[vmem] * 5 + [pl.BlockSpec(memory_space=pl.ANY)],
        out_specs=(vmem, vmem),
        scratch_shapes=[
            pltpu.VMEM((n_dev, mine, dim), BF16),
            pltpu.VMEM((n_dev, mine, classes), BF16),
            pltpu.VMEM((n_rows, dim), BF16),
            pltpu.VMEM((8, n_rows), F32),
            pltpu.VMEM((n_grp, 2 * q, CAP), BF16),
            pltpu.VMEM((n_grp, 2 * q, CAP), BF16),
            pltpu.VMEM((n_grp, 8, CAP), F32),
            pltpu.VMEM((n_grp, 8, CAP), F32),
            pltpu.VMEM((batch, 2 * q), F32),
            pltpu.VMEM((n_blk, piece, q), F32),
            pltpu.VMEM((n_blk, piece, q), F32),
            pltpu.VMEM((piece, q), F32),
            pltpu.VMEM((n_grp, piece, q), F32),
            pltpu.VMEM((n_blk, piece, q), F32),
            dma,
            dma((n_dev,)),
            dma((n_dev,)),
            dma((n_dev,)),
            dma((n_dev,)),
            dma((n_grp,)),
            dma((n_grp,)),
            dma((n_grp,)),
            dma((n_grp,)),
            dma((n_blk,)),
            dma((n_blk,)),
            dma((n_grp,)),
            dma((n_grp,)),
            dma((n_blk,)),
            dma((n_blk,)),
        ],
        compiler_params=pltpu.CompilerParams(
            collective_id=0, has_side_effects=True, vmem_limit_bytes=58 * 2**20
        ),
        cost_estimate=pl.CostEstimate(
            flops=2 * batch * n_rows * (dim + 2 * q), bytes_accessed=2 * n_rows * dim, transcendentals=batch * n_rows
        ),
    )(batch_x, grad, eigvec, eig_scale.reshape(1, q), sub_index.reshape(1, subs), centres)
    out = lax.dot_general(gp, rhs, (((0,), (0,)), ((), ())), preferred_element_type=F32)
    return out.T


def solution(mesh):
    grid = (mesh.shape["blk"], mesh.shape["group"])
    rows = P(("blk", "group"), None)
    in_specs = (rows, rows, rows, rows, P(), P(("blk", "group")))
    return jax.shard_map(
        functools.partial(body, grid), mesh=mesh, in_specs=in_specs, out_specs=rows, check_vma=False
    )
```

```python
import functools

import jax
import jax.numpy as jnp
from jax import lax
from jax.experimental import pallas as pl
from jax.experimental.pallas import tpu as pltpu
from jax.sharding import PartitionSpec as P

CAP = 128
TILE = 256
WIDE = 1024
F32, BF16 = jnp.float32, jnp.bfloat16


def nt(a, b):
    return lax.dot_general(a, b, (((1,), (1,)), ((), ())), preferred_element_type=F32)


def split(a):
    hi = a.astype(BF16)
    return hi, (a - hi.astype(F32)).astype(BF16)


def onehot(a, b):
    return jnp.where(a == b, 1.0, 0.0).astype(BF16)


def copy_to(src, dst, send, recv, blk, grp):
    return pltpu.make_async_remote_copy(
        src_ref=src,
        dst_ref=dst,
        send_sem=send,
        recv_sem=recv,
        device_id=(blk, grp),
        device_id_type=pl.DeviceIdType.MESH,
    )


class Gather:
    def __init__(self, me, grid, own, whole, send, recv):
        self.me, self.grid, self.own, self.whole, self.send, self.recv = me, grid, own, whole, send, recv
        self.sent = []

    def push(self, src, slot, blk, grp):
        copy = copy_to(src, self.whole.at[slot], self.send.at[len(self.sent)], self.recv.at[slot], blk, grp)
        copy.start()
        self.sent.append(copy)

    def wait(self, slot):
        blk, grp = self.me
        there = self.whole.at[slot]
        copy_to(there, there, self.send.at[0], self.recv.at[slot], self.twin, grp).wait_recv()

    @property
    def twin(self):
        blk, _ = self.me
        return blk + 1 - 2 * lax.rem(blk, 2)

    def chips(self):
        blk, _ = self.me
        n = self.grid[0] // 2
        core, chip = lax.rem(blk, 2), lax.div(blk, 2)
        return [2 * lax.rem(chip + k, n) + core for k in range(1, n)]

    def groups(self):
        _, grp = self.me
        return [lax.rem(grp + k, self.grid[1]) for k in range(1, self.grid[1])]

    def slot(self, blk, grp):
        return blk * self.grid[1] + grp

    def first(self):
        blk, grp = self.me
        slot = self.slot(blk, grp)
        self.whole[slot] = self.own[...]
        for other in self.groups():
            self.push(self.own, slot, blk, other)
        for other in self.chips():
            self.push(self.own, slot, other, grp)
        self.push(self.own, slot, self.twin, grp)

    def second(self):
        blk, grp = self.me
        for source in self.groups():
            slot = self.slot(blk, source)
            self.wait(slot)
            for other in self.chips():
                self.push(self.whole.at[slot], slot, other, grp)
            self.push(self.whole.at[slot], slot, self.twin, grp)

    def third(self):
        _, grp = self.me
        for source in [grp] + self.groups():
            for other in self.chips():
                slot = self.slot(other, source)
                self.wait(slot)
                self.push(self.whole.at[slot], slot, self.twin, grp)

    def last(self):
        _, grp = self.me
        n = self.grid[0] // 2
        core = lax.rem(self.twin, 2)
        for chip in range(n):
            for source in range(self.grid[1]):
                self.wait(self.slot(2 * chip + core, source))

    def drain(self):
        for copy in self.sent:
            copy.wait_send()


def exchange(
    grid, x_ref, g_ref, vec_ref, scale_ref, index_ref, c_hbm, gp_hbm, rhs_hbm,
    gp_ref, rhs_ref,
    xall, gall, cbuf, csq, vec_out, vec_in, row_out, row_in, acc,
    part, part_in, some, some_in, full, gown,
    c_sem, o_sem, x_send, x_recv, g_send, g_recv, v_send, v_recv, r_send, r_recv,
    p_send, p_recv, s_send, s_recv, f_send, f_recv,
):
    n_blk, n_grp = grid
    blk, grp = lax.axis_index("blk"), lax.axis_index("group")
    n_rows, dim = cbuf.shape
    subs = vec_ref.shape[0]
    q = vec_ref.shape[1]
    batch = xall.shape[0] * xall.shape[1]
    piece = batch // n_blk
    classes = g_ref.shape[1]
    wide = gown.shape[1]
    tiles = n_rows // TILE

    load = pltpu.make_async_copy(c_hbm, cbuf, c_sem)
    load.start()
    gown[...] = jnp.zeros_like(gown)
    gown[:, :classes] = g_ref[...]

    other_grps = [lax.rem(grp + k, n_grp) for k in range(1, n_grp)]
    other_blks = [lax.rem(blk + k, n_blk) for k in range(1, n_blk)]
    barrier = pltpu.get_barrier_semaphore()
    for other in other_grps:
        pl.semaphore_signal(barrier, inc=1, device_id=(blk, other), device_id_type=pl.DeviceIdType.MESH)
    for other in other_blks:
        pl.semaphore_signal(barrier, inc=1, device_id=(other, grp), device_id_type=pl.DeviceIdType.MESH)
    pl.semaphore_wait(barrier, n_grp + n_blk - 2)

    xs = Gather((blk, grp), grid, x_ref, xall, x_send, x_recv)
    gs = Gather((blk, grp), grid, gown, gall, g_send, g_recv)
    xs.first()

    index = jnp.broadcast_to(index_ref[...], (8, subs))
    shift = n_rows.bit_length() - 1
    local = index & (n_rows - 1)
    holder = lax.shift_right_logical(index, shift) & (n_grp - 1)
    line = lax.broadcasted_iota(jnp.int32, (8, subs), 0)
    member = jnp.where(holder == line, 1.0, 0.0)
    upper = jnp.where(
        lax.broadcasted_iota(jnp.int32, (subs, subs), 0) < lax.broadcasted_iota(jnp.int32, (subs, subs), 1), 1.0, 0.0
    ).astype(BF16)
    order = jnp.sum(member * jnp.dot(member.astype(BF16), upper, preferred_element_type=F32), axis=0, keepdims=True)
    position = holder[0:1].astype(F32) * CAP + order
    places = n_grp * CAP
    select = onehot(lax.broadcasted_iota(jnp.int32, (places, subs), 0).astype(F32), position)
    vec_hi, vec_lo = split(vec_ref[...])
    table = jnp.dot(select, jnp.concatenate([vec_hi, vec_lo], axis=1), preferred_element_type=F32).T
    wanted = jnp.where(line == 0, lax.shift_right_logical(local, 7), jnp.where(line == 1, local & 127, 1))
    rows = nt(wanted.astype(F32).astype(BF16), select)
    for k in range(n_grp):
        vec_out[k] = table[:, k * CAP : (k + 1) * CAP].astype(BF16)
        row_out[k] = rows[:, k * CAP : (k + 1) * CAP]
    vecs = []
    for k, other in enumerate(other_grps):
        vecs.append(copy_to(vec_out.at[other], vec_in.at[grp], v_send.at[k], v_recv.at[grp], blk, other))
        vecs.append(copy_to(row_out.at[other], row_in.at[grp], r_send.at[k], r_recv.at[grp], blk, other))
    for copy in vecs:
        copy.start()
    vec_in[grp] = vec_out[grp]
    row_in[grp] = row_out[grp]

    xs.second()
    gs.first()

    load.wait()
    ones = jnp.ones((8, 128), BF16)

    @pl.loop(0, tiles)
    def _(t):
        block = cbuf[pl.ds(pl.multiple_of(t * TILE, TILE), TILE), :].astype(F32)
        square = block * block
        total = square[:, :128]
        for k in range(1, dim // 128):
            total = total + square[:, k * 128 : (k + 1) * 128]
        hi = total.astype(BF16)
        mid, low = split(total - hi.astype(F32))
        csq[:, pl.ds(pl.multiple_of(t * TILE, TILE), TILE)] = nt(ones, hi) + nt(ones, mid) + nt(ones, low)

    xs.third()
    gs.second()

    for other in other_grps:
        copy_to(vec_in.at[other], vec_in.at[other], v_send.at[0], v_recv.at[other], blk, other).wait_recv()
        copy_to(row_in.at[other], row_in.at[other], r_send.at[0], r_recv.at[other], blk, other).wait_recv()
    vec_all = jnp.concatenate([vec_in[k] for k in range(n_grp)], axis=1)
    rows = jnp.concatenate([row_in[k] for k in range(n_grp)], axis=1)
    place = rows[0:1] * 128.0 + rows[1:2] + (rows[2:3] - 1.0) * (2.0 * n_rows)

    @pl.loop(0, tiles)
    def _(t):
        where = (lax.broadcasted_iota(jnp.int32, (TILE, places), 0) + t * TILE).astype(F32)
        at_centres = nt(vec_all, onehot(where, place)).astype(BF16)
        columns = pl.ds(pl.multiple_of(t * TILE, TILE), TILE)
        rhs_ref[batch : batch + 2 * q, columns] = at_centres

    xs.last()
    x = xall[...].reshape(batch, dim)
    xf = x.astype(F32)
    bsq = jnp.sum(xf * xf, axis=1, keepdims=True)
    acc[...] = jnp.zeros_like(acc)

    @pl.loop(0, n_rows // WIDE)
    def _(t):
        columns = pl.ds(pl.multiple_of(t * WIDE, WIDE), WIDE)
        inner = nt(xall[...].reshape(batch, dim), cbuf[columns, :])
        distance = csq[0:1, columns] + bsq - 2.0 * inner
        kern = jnp.exp(distance * (-0.5 / dim)).astype(BF16)
        rhs_ref[0:batch, columns] = kern
        acc[...] += nt(kern, rhs_ref[batch : batch + 2 * q, columns])

    both = acc[:, :q] + acc[:, q:]
    for k in range(n_blk):
        part[k] = both[k * piece : (k + 1) * piece]
    parts = [
        copy_to(part.at[other], part_in.at[blk], p_send.at[k], p_recv.at[blk], other, grp)
        for k, other in enumerate(other_blks)
    ]
    for copy in parts:
        copy.start()
    part_in[blk] = part[blk]
    right = pltpu.make_async_copy(rhs_ref, rhs_hbm, o_sem.at[0])
    right.start()
    gs.third()
    for other in other_blks:
        copy_to(part_in.at[other], part_in.at[other], p_send.at[0], p_recv.at[other], other, grp).wait_recv()
    some[...] = functools.reduce(jnp.add, [part_in[k] for k in range(n_blk)])
    somes = [
        copy_to(some, some_in.at[grp], s_send.at[k], s_recv.at[grp], blk, other) for k, other in enumerate(other_grps)
    ]
    for copy in somes:
        copy.start()
    some_in[grp] = some[...]
    gs.last()

    @pl.loop(0, wide // TILE)
    def _(t):
        columns = pl.ds(pl.multiple_of(t * TILE, TILE), TILE)
        gp_ref[columns, 0:batch] = gall[:, :, columns].reshape(batch, TILE).astype(F32).T.astype(BF16)

    left = pltpu.make_async_copy(gp_ref.at[:, 0:batch], gp_hbm.at[:, 0:batch], o_sem.at[1])
    left.start()
    for other in other_grps:
        copy_to(some_in.at[other], some_in.at[other], s_send.at[0], s_recv.at[other], blk, other).wait_recv()
    full[blk] = functools.reduce(jnp.add, [some_in[k] for k in range(n_grp)]).astype(BF16)
    fulls = [
        copy_to(full.at[blk], full.at[blk], f_send.at[k], f_recv.at[blk], other, grp)
        for k, other in enumerate(other_blks)
    ]
    for copy in fulls:
        copy.start()
    for other in other_blks:
        copy_to(full.at[other], full.at[other], f_send.at[0], f_recv.at[other], other, grp).wait_recv()

    product = jnp.dot(gp_ref[:, 0:batch], full[...].reshape(batch, q), preferred_element_type=F32)
    hi = (product * -scale_ref[...]).astype(BF16)
    gp_ref[:, batch : batch + q] = hi
    gp_ref[:, batch + q : batch + 2 * q] = hi

    rest = pltpu.make_async_copy(gp_ref.at[:, batch:], gp_hbm.at[:, batch:], o_sem.at[2])
    rest.start()
    xs.drain()
    gs.drain()
    for copy in vecs + parts + somes + fulls:
        copy.wait_send()
    for copy in (right, left, rest):
        copy.wait()


def final(gp_hbm, rhs_hbm, out_hbm, gp, rhs, out, gp_sem, rhs_sem, out_sem):
    classes = out.shape[0]
    tiles = rhs.shape[1] // WIDE

    def left(k):
        rows = pl.ds(k * TILE, TILE)
        return pltpu.make_async_copy(gp_hbm.at[rows], gp.at[rows], gp_sem.at[k])

    def column(t):
        return pl.ds(pl.multiple_of(t * WIDE, WIDE), WIDE)

    def right(t):
        return pltpu.make_async_copy(rhs_hbm.at[:, column(t)], rhs.at[:, column(t)], rhs_sem.at[t])

    def result(t):
        return pltpu.make_async_copy(out.at[:, column(t)], out_hbm.at[:, column(t)], out_sem.at[t])

    right(0).start()
    for k in range(gp.shape[0] // TILE):
        left(k).start()
    for t in range(1, tiles):
        right(t).start()
    for k in range(gp.shape[0] // TILE):
        left(k).wait()

    @pl.loop(0, tiles)
    def _(t):
        right(t).wait()
        out[:, column(t)] = jnp.dot(gp[...], rhs[:, column(t)], preferred_element_type=F32)[:classes]
        result(t).start()

    @pl.loop(0, tiles)
    def _(t):
        result(t).wait()


def body(grid, centres, batch_x, grad, eigvec, eig_scale, sub_index):
    n_blk, n_grp = grid
    n_dev = n_blk * n_grp
    n_rows, dim = centres.shape
    mine, classes = grad.shape
    subs, q = eigvec.shape
    batch = mine * n_dev
    piece = batch // n_blk
    wide = pl.cdiv(classes, TILE) * TILE
    deep = batch + 2 * q
    dma = pltpu.SemaphoreType.DMA
    vmem = pl.BlockSpec(memory_space=pltpu.VMEM)
    anywhere = pl.BlockSpec(memory_space=pl.ANY)
    gp, rhs = pl.pallas_call(
        functools.partial(exchange, grid),
        out_shape=(
            jax.ShapeDtypeStruct((wide, deep), BF16),
            jax.ShapeDtypeStruct((deep, n_rows), BF16),
        ),
        in_specs=[vmem] * 5 + [anywhere],
        out_specs=(anywhere, anywhere),
        scratch_shapes=[
            pltpu.VMEM((wide, deep), BF16),
            pltpu.VMEM((deep, n_rows), BF16),
            pltpu.VMEM((n_dev, mine, dim), BF16),
            pltpu.VMEM((n_dev, mine, wide), BF16),
            pltpu.VMEM((n_rows, dim), BF16),
            pltpu.VMEM((8, n_rows), F32),
            pltpu.VMEM((n_grp, 2 * q, CAP), BF16),
            pltpu.VMEM((n_grp, 2 * q, CAP), BF16),
            pltpu.VMEM((n_grp, 8, CAP), F32),
            pltpu.VMEM((n_grp, 8, CAP), F32),
            pltpu.VMEM((batch, 2 * q), F32),
            pltpu.VMEM((n_blk, piece, q), F32),
            pltpu.VMEM((n_blk, piece, q), F32),
            pltpu.VMEM((piece, q), F32),
            pltpu.VMEM((n_grp, piece, q), F32),
            pltpu.VMEM((n_blk, piece, q), BF16),
            pltpu.VMEM((mine, wide), BF16),
            dma,
            dma((3,)),
            dma((n_dev,)),
            dma((n_dev,)),
            dma((n_dev,)),
            dma((n_dev,)),
            dma((n_grp,)),
            dma((n_grp,)),
            dma((n_grp,)),
            dma((n_grp,)),
            dma((n_blk,)),
            dma((n_blk,)),
            dma((n_grp,)),
            dma((n_grp,)),
            dma((n_blk,)),
            dma((n_blk,)),
        ],
        compiler_params=pltpu.CompilerParams(
            collective_id=0, has_side_effects=True, vmem_limit_bytes=58 * 2**20
        ),
        cost_estimate=pl.CostEstimate(
            flops=2 * batch * n_rows * (dim + 2 * q), bytes_accessed=2 * n_rows * dim, transcendentals=batch * n_rows
        ),
    )(batch_x, grad, eigvec, eig_scale.reshape(1, q), sub_index.reshape(1, subs), centres)
    out = pl.pallas_call(
        final,
        out_shape=jax.ShapeDtypeStruct((classes, n_rows), F32),
        in_specs=[anywhere, anywhere],
        out_specs=anywhere,
        scratch_shapes=[
            pltpu.VMEM((wide, deep), BF16),
            pltpu.VMEM((deep, n_rows), BF16),
            pltpu.VMEM((classes, n_rows), F32),
            dma((wide // TILE,)),
            dma((n_rows // WIDE,)),
            dma((n_rows // WIDE,)),
        ],
        compiler_params=pltpu.CompilerParams(vmem_limit_bytes=60 * 2**20),
        cost_estimate=pl.CostEstimate(
            flops=2 * wide * deep * n_rows, bytes_accessed=4 * classes * n_rows, transcendentals=0
        ),
    )(gp, rhs)
    return out.T


def solution(mesh):
    grid = (mesh.shape["blk"], mesh.shape["group"])
    rows = P(("blk", "group"), None)
    in_specs = (rows, rows, rows, rows, P(), P(("blk", "group")))
    return jax.shard_map(
        functools.partial(body, grid), mesh=mesh, in_specs=in_specs, out_specs=rows, check_vma=False
    )
```
